1024 devices in a mesh: pipe: 128 (over y_hi, z, core), dp: 8 (over x, y_lo).
Axes of the slice: x: 4, y: 4 (y_hi: 2, y_lo: 2; y = y_hi * 2 + y_lo), z: 32, core: 2. Of those that a mesh axis runs over, the one named last changes fastest.
Arguments:
- forward_state: bfloat16 [2, 128, 128, 3584], P(None, 'pipe', 'dp'), may hold values from -6 to 6
- backward_state: bfloat16 [2, 128, 128, 3584], P(None, 'pipe', 'dp'), may hold values from -1.5 to 1.5
- stored_inputs: bfloat16 [2, 128, 2, 128, 3584], P(None, 'pipe', None, 'dp'), may hold values from -6 to 6
- down_weight: bfloat16 [128, 2, 3584, 256], P('pipe'), may hold values from -0.09375 to 0.09375
- up_weight: bfloat16 [128, 2, 256, 3584], P('pipe'), may hold values from -0.375 to 0.375
- norm_gain: float32 [128, 2, 3584], P('pipe'), may hold values from 0.25 to 1.75
- latent_gain: float32 [128, 2, 2, 256], P('pipe'), may hold values from 0.25 to 1.75
- forward_lengths: int32 [2, 128, 4, 8], P(None, 'pipe', None, 'dp'), may hold values from 1 to 16
- stored_lengths: int32 [2, 128, 2, 8], P(None, 'pipe', None, 'dp'), may hold values from 1 to 16
- plan: int32 [2, 128, 4], P(None, 'pipe'), may hold values from 0 to 1
Outputs:
- forward_out: bfloat16 [2, 128, 128, 3584], P(None, 'pipe', 'dp')
- backward_out: bfloat16 [2, 128, 128, 3584], P(None, 'pipe', 'dp')
- grad_down: float32 [128, 3584, 256], P('pipe', 'dp')
The draws below stay inside these ranges and needn't reach their ends.
Inputs may be any that keep to these rules, and one draw needn't show every extreme that they name: `forward_lengths`: valid tokens of a forward micro-batch. `stored_lengths`: valid tokens of a stored micro-batch. `plan`: a slot of the stored inputs.
All inputs are finite; a program needn't handle non-finite values.
Results may differ from the reference program's by a relative error of at most 0.027.
Values may be sent and summed in bfloat16 or wider, within the bound.
No kernel may reach another device: no remote copies, remote signals or barrier semaphores. Data moves between devices by JAX's collectives and lax.ppermute only.
A program may use at most 64 MiB of HBM per device.

```python
import jax
import jax.numpy as jnp
from jax import lax

D = 3584
C = 256
MBT = 16
TICKS = 4
SLOTS = 2
TOKENS = 128
N_PIPE = 128
N_DP = 8


def touch_ends(entries, rng, smallest, largest):
    dims = entries.shape
    place = [jax.random.randint(jax.random.fold_in(rng, axis), (), 0, dims[axis]) for axis in range(len(dims))]
    entries = entries.at[tuple(place)].set(smallest)
    longest = dims.index(max(dims))
    place[longest] = (place[longest] + 1) % dims[longest]
    return entries.at[tuple(place)].set(largest)


def levels(rng, dims, shards, low, largest):
    def one(axis_at, parts):
        heights = jax.random.uniform(jax.random.fold_in(jax.random.fold_in(rng, 6), axis_at), (parts,), jnp.float32, low / len(shards), largest / len(shards))
        return jnp.repeat(jnp.exp(heights), dims[axis_at] // parts).reshape((-1,) + (1,) * (len(dims) - axis_at - 1))

    factor_of = one(*shards[0])
    for cut in shards[1:]:
        factor_of = factor_of * one(*cut)
    return factor_of


def bell_draw(key, shape, scale, most, split=(), held_as=jnp.bfloat16):
    values = jax.random.normal(key, shape, jnp.float32) * scale
    if len(split) > 0:
        values = levels(key, shape, split, -0.22, 0.18) * values
    return jnp.clip(values, min=-most, max=most).astype(held_as)


def setup_inputs(seed: int = 0) -> dict:
    key_list = jax.random.split(jax.random.key(seed), 11)
    return {
        "forward_state": bell_draw(key_list[0], (2, N_PIPE, TOKENS, D), 1.0, 6.0, ((1, 128), (2, 8))),
        "backward_state": bell_draw(key_list[1], (2, N_PIPE, TOKENS, D), 0.25, 1.5, ((1, 128), (2, 8))),
        "stored_inputs": bell_draw(key_list[2], (2, N_PIPE, SLOTS, TOKENS, D), 1.0, 6.0, ((1, 128), (3, 8))),
        "down_weight": bell_draw(key_list[3], (N_PIPE, 2, D, C), D ** -0.5, 0.09375, ((0, 128),)),
        "up_weight": bell_draw(key_list[4], (N_PIPE, 2, C, D), C ** -0.5, 0.375, ((0, 128),)),
        "norm_gain": jnp.clip(1.0 + 0.15 * jax.random.normal(key_list[5], (N_PIPE, 2, D), jnp.float32), 0.25, 1.75),
        "latent_gain": jnp.clip(1.0 + 0.15 * jax.random.normal(key_list[6], (N_PIPE, 2, 2, C), jnp.float32), 0.25, 1.75),
        "forward_lengths": touch_ends(jax.random.randint(key_list[7], (2, N_PIPE, TICKS, N_DP), 1, MBT + 1), jax.random.fold_in(key_list[7], 1), 1, MBT).astype(jnp.int32),
        "stored_lengths": touch_ends(jax.random.randint(key_list[8], (2, N_PIPE, SLOTS, N_DP), 1, MBT + 1), jax.random.fold_in(key_list[8], 1), 1, MBT).astype(jnp.int32),
        "plan": touch_ends(jax.random.randint(key_list[9], (2, N_PIPE, TICKS), 0, SLOTS), jax.random.fold_in(key_list[9], 1), 0, SLOTS - 1).astype(jnp.int32),
    }


epsilon = 1e-06
score_factor = 2.0

def round_through(values):
    rounded = values.astype(jnp.bfloat16).astype(jnp.float32)
    return values + lax.stop_gradient(rounded - values)

def normed_input(inputs_float, gain_vector):
    inverse = lax.rsqrt(lax.optimization_barrier(jnp.mean(inputs_float * inputs_float, axis=-1, keepdims=True)) + epsilon)
    return inputs_float * inverse * gain_vector

def attend(latent, latent_gain, length):
    row_count = latent.shape[1]
    inverse = lax.rsqrt(lax.optimization_barrier(jnp.mean(latent * latent, axis=-1, keepdims=True)) + epsilon)
    key_rows = round_through(latent * inverse * latent_gain[0])
    query_rows = round_through(latent * inverse * latent_gain[1])
    scores = jnp.einsum('gic,gjc->gij', query_rows, key_rows, precision=lax.Precision.HIGHEST) * (score_factor / latent.shape[2])
    position = jnp.arange(row_count)
    visible = (position[None, None, :] <= position[None, :, None]) & (position[None, None, :] < length[:, None, None])
    weights = jnp.where(visible, jnp.exp(scores), 0.0)
    probabilities = round_through(weights / lax.optimization_barrier(jnp.sum(weights, axis=-1, keepdims=True)))
    return round_through(jnp.einsum('gij,gjc->gic', probabilities, key_rows, precision=lax.Precision.HIGHEST))

def segment_forward(inputs, w_down, w_up, gain_vector, latent_gain, length):
    groups, row_count, features = inputs.shape
    inputs_float = inputs.astype(jnp.float32)
    normed = normed_input(inputs_float, gain_vector).astype(jnp.bfloat16)
    latent = jnp.dot(normed.reshape(groups * row_count, features), w_down, preferred_element_type=jnp.float32)
    mixed_rows = attend(latent.reshape(groups, row_count, -1), latent_gain, length).astype(jnp.bfloat16)
    update = jnp.dot(mixed_rows.reshape(groups * row_count, -1), w_up, preferred_element_type=jnp.float32)
    return (inputs_float + update.reshape(inputs.shape)).astype(jnp.bfloat16)

def segment_backward(inputs, grad_out, w_down, w_up, gain_vector, latent_gain, length):
    groups, row_count, features = inputs.shape
    inputs_float = inputs.astype(jnp.float32)
    normed = normed_input(inputs_float, gain_vector).astype(jnp.bfloat16)
    flat_normed = normed.reshape(groups * row_count, features)
    latent = jnp.dot(flat_normed, w_down, preferred_element_type=jnp.float32)
    flat_grad = grad_out.reshape(groups * row_count, features)
    grad_mixed = jnp.dot(flat_grad, w_up.T, preferred_element_type=jnp.float32)
    _, pull_latent = jax.vjp(lambda latent_rows: attend(latent_rows, latent_gain, length), latent.reshape(groups, row_count, -1))
    grad_latent = pull_latent(grad_mixed.reshape(groups, row_count, -1))[0].reshape(groups * row_count, -1).astype(jnp.bfloat16)
    grad_normed = jnp.dot(grad_latent, w_down.T, preferred_element_type=jnp.float32)
    _, pull_norm = jax.vjp(lambda values: normed_input(values, gain_vector), inputs_float)
    grad_input = grad_out.astype(jnp.float32) + pull_norm(grad_normed.reshape(inputs.shape))[0]
    return (grad_input.astype(jnp.bfloat16), flat_normed, grad_latent)

def reference(forward_state, backward_state, stored_inputs, down_weight, up_weight, norm_gain, latent_gain, forward_lengths, stored_lengths, plan):
    replicas = forward_lengths.shape[3]
    batch_rows = forward_state.shape[2] // replicas
    features = forward_state.shape[3]
    forward = [forward_state[0], forward_state[1]]
    backward = [backward_state[0], backward_state[1]]
    kept_normed = [[], []]
    kept_grads = [[], []]
    for step_index in range(TICKS):
        moved_forward = []
        moved_backward = []
        for side_index in range(2):

            def one_forward(operands):
                inputs, w_down, w_up, gain_vector, gains_latent, length = operands
                result = segment_forward(inputs.reshape(replicas, batch_rows, features), w_down, w_up, gain_vector, gains_latent, length)
                return result.reshape(replicas * batch_rows, features)
            outputs = lax.map(one_forward, (forward[side_index], down_weight[:, side_index], up_weight[:, side_index], norm_gain[:, side_index], latent_gain[:, side_index], forward_lengths[side_index, :, step_index]))

            def one_backward(operands):
                stored, stored_len, slot_index, grad_out, w_down, w_up, gain_vector, gains_latent = operands
                chosen = lax.dynamic_index_in_dim(stored, slot_index, 0, keepdims=False)
                length = lax.dynamic_index_in_dim(stored_len, slot_index, 0, keepdims=False)
                grad_input, normed, grad_latent = segment_backward(chosen.reshape(replicas, batch_rows, features), grad_out.reshape(replicas, batch_rows, features), w_down, w_up, gain_vector, gains_latent, length)
                return (grad_input.reshape(replicas * batch_rows, features), normed.reshape(replicas, batch_rows, features), grad_latent.reshape(replicas, batch_rows, -1))
            grad_input, normed, grad_latent = lax.map(one_backward, (stored_inputs[side_index], stored_lengths[side_index], plan[side_index, :, step_index], backward[side_index], down_weight[:, side_index], up_weight[:, side_index], norm_gain[:, side_index], latent_gain[:, side_index]))
            kept_normed[side_index].append(normed)
            kept_grads[side_index].append(grad_latent)
            zero_rows = jnp.zeros_like(outputs[:1])
            if side_index == 0:
                moved_forward.append(jnp.concatenate([zero_rows, outputs[:-1]], axis=0))
                moved_backward.append(jnp.concatenate([grad_input[1:], zero_rows], axis=0))
            else:
                moved_forward.append(jnp.concatenate([outputs[1:], zero_rows], axis=0))
                moved_backward.append(jnp.concatenate([zero_rows, grad_input[:-1]], axis=0))
        forward = moved_forward
        backward = moved_backward
    normed_lower = jnp.concatenate(kept_normed[0], axis=2)
    grads_lower = jnp.concatenate(kept_grads[0], axis=2)
    normed_upper = jnp.concatenate(kept_normed[1], axis=2)[::-1]
    grads_upper = jnp.concatenate(kept_grads[1], axis=2)[::-1]
    normed_both = jnp.concatenate([normed_lower, normed_upper], axis=2)
    grads_both = jnp.concatenate([grads_lower, grads_upper], axis=2)

    def one_sum(operands):
        normed_rows, grad_rows = operands
        partial_value = jnp.einsum('rtd,rtc->rdc', normed_rows.astype(jnp.float32), grad_rows.astype(jnp.float32))
        rounded = lax.optimization_barrier(partial_value.astype(jnp.bfloat16)).astype(jnp.float32)
        return lax.optimization_barrier(jnp.sum(rounded, axis=0))
    grad_down = lax.map(one_sum, (normed_both, grads_both))
    return (jnp.stack(forward), jnp.stack(backward), grad_down)
```

```python
import functools

import jax
import jax.numpy as jnp
from jax import lax
from jax.experimental import pallas as pl
from jax.experimental.pallas import tpu as pltpu
from jax.sharding import PartitionSpec as P

epsilon = 1e-06
score_factor = 2.0
vmem_limit = 12 * 1024 * 1024


def with_chip_partner(block):
    count = lax.axis_size("pipe")
    return lax.ppermute(block, "pipe", [(i, i ^ 1) for i in range(count)])


def with_outer_partner(block):
    count = lax.axis_size("pipe")
    pairs = []
    for low in range(1, count - 1, 2):
        pairs += [(low, low + 1), (low + 1, low)]
    return lax.ppermute(block, "pipe", pairs)


def from_mirror(block):
    count = lax.axis_size("pipe")
    return lax.ppermute(block, "pipe", [(i, count - 1 - i) for i in range(count)])


def contract(left, right, left_dim, right_dim):
    return lax.dot_general(
        left, right, (((left_dim,), (right_dim,)), ((), ())), preferred_element_type=jnp.float32
    )


def inverse_rms(values):
    return lax.rsqrt(jnp.mean(values * values, axis=-1, keepdims=True) + epsilon)


def probabilities_of(query_rows, key_rows, length):
    row_count, width = query_rows.shape
    scores = contract(query_rows, key_rows, 1, 1) * (score_factor / width)
    query_at = lax.broadcasted_iota(jnp.int32, (row_count, row_count), 0)
    key_at = lax.broadcasted_iota(jnp.int32, (row_count, row_count), 1)
    visible = (key_at <= query_at) & (key_at < length)
    weights = jnp.where(visible, jnp.exp(scores), 0.0)
    return weights / jnp.sum(weights, axis=-1, keepdims=True)


def prepare_kernel(
    place,
    forward_lengths,
    plan,
    stored_lengths,
    stored,
    forward_state,
    backward_state,
    w_down,
    gain,
    latent_gain,
    scalars_out,
    normed_out,
    to_mirror_out,
    inner_out,
    outer_out,
    grads_zero_out,
    grads_one_out,
    key_out,
    query_out,
    unit_out,
    latent_inverse_out,
    input_inverse_out,
    probabilities_out,
    weights,
    stored_here,
    gain_here,
    latent_gain_here,
    forward_lengths_here,
    plan_here,
    stored_lengths_here,
    weights_arrived,
    inputs_arrived,
    states_arrived,
    numbers_arrived,
    *,
    forward_lengths_at,
    plan_at,
):
    sides, slots, row_count = probabilities_out.shape[:3]
    replicas, block, columns = normed_out.shape
    steps = plan.shape[2]
    core = place[0]
    copies = [
        pltpu.make_async_copy(w_down.at[side], weights.at[side], weights_arrived.at[side])
        for side in range(sides)
    ]
    inputs = [
        pltpu.make_async_copy(source, target, inputs_arrived.at[at])
        for at, (source, target) in enumerate(
            ((gain, gain_here), (stored, stored_here), (latent_gain, latent_gain_here))
        )
    ]
    others = [
        pltpu.make_async_copy(source, target, numbers_arrived.at[at])
        for at, (source, target) in enumerate(
            (
                (forward_lengths, forward_lengths_here),
                (plan, plan_here),
                (stored_lengths, stored_lengths_here),
            )
        )
    ]
    others += [
        pltpu.make_async_copy(source.at[side], target, states_arrived.at[at])
        for at, (source, side, target) in enumerate(
            (
                (forward_state, 1 - core, inner_out.at[0:row_count]),
                (backward_state, core, inner_out.at[row_count : 2 * row_count]),
                (forward_state, core, outer_out.at[0:row_count]),
                (backward_state, 1 - core, outer_out.at[row_count : 2 * row_count]),
            )
        )
    ]
    for copy in inputs + copies + others:
        copy.start()
    grads_zero_out[...] = jnp.zeros(grads_zero_out.shape, grads_zero_out.dtype)
    grads_one_out[...] = jnp.zeros(grads_one_out.shape, grads_one_out.dtype)
    for copy in inputs:
        copy.wait()
    all_normed = []
    for side in range(sides):
        rows = stored_here[side].astype(jnp.float32)
        inverse = inverse_rms(rows)
        input_inverse_out[side] = jnp.broadcast_to(inverse, input_inverse_out.shape[1:])
        normed = (rows * inverse * gain_here[side : side + 1]).astype(jnp.bfloat16)
        all_normed.append(normed)
        for replica in range(replicas):
            part = normed[:, replica * columns : (replica + 1) * columns]
            (normed_out, to_mirror_out)[side][replica] = part
    for copy in others:
        copy.wait()
    scalars_out[0] = core
    for side in range(sides):
        for step in range(steps):
            scalars_out[forward_lengths_at + side * steps + step] = forward_lengths_here[
                side, 0, 0, step
            ]
            scalars_out[plan_at + side * steps + step] = plan_here[side, 0, step]
    for side in range(sides):
        copies[side].wait()
        latent = jnp.dot(all_normed[side], weights[side], preferred_element_type=jnp.float32)
        inverse = inverse_rms(latent)
        unit = latent * inverse
        key_rows = (unit * latent_gain_here[side, 0:1]).astype(jnp.bfloat16)
        query_rows = (unit * latent_gain_here[side, 1:2]).astype(jnp.bfloat16)
        latent_inverse_out[side] = jnp.broadcast_to(inverse, latent_inverse_out.shape[1:])
        unit_out[side] = unit
        key_out[side] = key_rows
        query_out[side] = query_rows
        for slot in range(slots):
            part = slice(slot * row_count, (slot + 1) * row_count)
            probabilities_out[side, slot] = probabilities_of(
                query_rows[part], key_rows[part], stored_lengths_here[side, 0, 0, slot]
            )


def normed_rows(rows, gain_row):
    return (rows * inverse_rms(rows) * gain_row).astype(jnp.bfloat16)


def forward_ended(rows, latent, side, length, w_up, latent_gain):
    unit = latent * inverse_rms(latent)
    gains = latent_gain[side]
    key_rows = (unit * gains[0:1]).astype(jnp.bfloat16)
    query_rows = (unit * gains[1:2]).astype(jnp.bfloat16)
    weights = probabilities_of(query_rows, key_rows, length).astype(jnp.bfloat16)
    mixed_rows = jnp.dot(weights, key_rows, preferred_element_type=jnp.float32)
    update = jnp.dot(
        mixed_rows.astype(jnp.bfloat16), w_up[side], preferred_element_type=jnp.float32
    )
    return (rows + update).astype(jnp.bfloat16)


def grad_latent_of(grad_mixed, side, slot, latent_gain, kept):
    keys, queries, units, latent_inverses, _, probabilities = kept
    row_count = grad_mixed.shape[0]
    mine = pl.ds(pl.multiple_of(slot * row_count, row_count), row_count)
    key_rows = keys[side, mine]
    query_rows = queries[side, mine]
    weights = probabilities[side, slot]
    gains = latent_gain[side]
    grad_mixed = grad_mixed.astype(jnp.bfloat16)
    grad_weights = contract(grad_mixed, key_rows, 1, 1)
    grad_scores = weights * (
        grad_weights - jnp.sum(grad_weights * weights, axis=-1, keepdims=True)
    )
    grad_scores = (grad_scores * (score_factor / key_rows.shape[1])).astype(jnp.bfloat16)
    grad_query = contract(grad_scores, key_rows, 1, 0)
    grad_key = contract(weights.astype(jnp.bfloat16), grad_mixed, 0, 0) + contract(
        grad_scores, query_rows, 0, 0
    )
    grad_unit = grad_key * gains[0:1] + grad_query * gains[1:2]
    unit = units[side, mine]
    return (
        latent_inverses[side, mine][:, 0:1]
        * (grad_unit - unit * jnp.mean(grad_unit * unit, axis=-1, keepdims=True))
    ).astype(jnp.bfloat16)


def backward_ended(grad_out, grad_latent, side, slot, stored, w_down, gain, kept):
    row_count = grad_out.shape[0]
    mine = pl.ds(pl.multiple_of(slot * row_count, row_count), row_count)
    grad_normed = contract(grad_latent, w_down[side], 1, 1)
    inverse = kept[4][side, mine][:, 0:1]
    unit = stored[side, mine].astype(jnp.float32) * inverse
    grad_unit = grad_normed * gain[pl.ds(side, 1)]
    grad_rows = inverse * (grad_unit - unit * jnp.mean(grad_unit * unit, axis=-1, keepdims=True))
    return (grad_out.astype(jnp.float32) + grad_rows).astype(jnp.bfloat16)


def of_slot(grad_latent, slot, slots):
    grad_latent = grad_latent.astype(jnp.float32)
    return jnp.concatenate(
        [jnp.where(slot == at, grad_latent, 0.0) for at in range(slots)], axis=0
    )


def half_step_kernel(
    scalars,
    arrived,
    stored,
    w_down,
    w_up,
    gain,
    latent_gain,
    *refs,
    forward_lane,
    lengths_at,
    plan_at,
    steps,
    step,
):
    kept, (grads_in, outgoing, grads_out) = refs[:6], refs[6:]
    row_count = outgoing.shape[0] // 2
    core = scalars[0]
    forward_side = forward_lane ^ core
    backward_side = 1 - forward_side
    slot = scalars[plan_at + backward_side * steps + step]
    length = scalars[lengths_at + forward_side * steps + step]
    rows = arrived[0:row_count].astype(jnp.float32)
    grad_out = arrived[row_count:]

    grad_mixed = contract(grad_out, w_up[backward_side], 1, 1)
    normed = normed_rows(rows, gain[pl.ds(forward_side, 1)])
    latent = jnp.dot(normed, w_down[forward_side], preferred_element_type=jnp.float32)
    grad_latent = grad_latent_of(grad_mixed, backward_side, slot, latent_gain, kept)
    grads_out[...] = grads_in[...] + of_slot(grad_latent, slot, grads_out.shape[0] // row_count)
    outgoing[0:row_count] = forward_ended(rows, latent, forward_side, length, w_up, latent_gain)
    outgoing[row_count:] = backward_ended(
        grad_out, grad_latent, backward_side, slot, stored, w_down, gain, kept
    )


def own_grads_kernel(place, grads_zero, grads_one, lower, upper):
    first = place[0] == 0
    lower[...] = jnp.where(first, grads_zero[...], grads_one[...]).astype(lower.dtype)
    upper[...] = jnp.where(first, grads_one[...], grads_zero[...]).astype(upper.dtype)


def own_states_kernel(place, inner, outer, forward_out, backward_out):
    core = place[0]
    row_count = forward_out.shape[1]
    forward_out[core] = outer[0:row_count]
    forward_out[1 - core] = inner[0:row_count]
    backward_out[core] = inner[row_count:]
    backward_out[1 - core] = outer[row_count:]


def pack_kernel(rows_lower, rows_upper, grads_lower, grads_upper, packed):
    replicas, block, columns = rows_lower.shape
    for replica in range(replicas):
        packed[replica, 0:block] = jnp.concatenate([rows_lower[replica], grads_lower[...]], axis=1)
        packed[replica, block:] = jnp.concatenate([rows_upper[replica], grads_upper[...]], axis=1)


def product_kernel(packed, result):
    replicas, block, width = packed.shape
    columns = result.shape[0]
    packed = packed[...].reshape(replicas * block, width)
    result[...] = contract(packed[:, :columns], packed[:, columns:], 0, 0)


def in_vmem(count):
    return [pl.BlockSpec(memory_space=pltpu.VMEM)] * count


def in_smem(count):
    return [pl.BlockSpec(memory_space=pltpu.SMEM)] * count


def like(*shape, dtype=jnp.float32):
    return jax.ShapeDtypeStruct(shape, dtype)


def call_kernel(kernel, outs, scalars, *operands, scalar_outs=0, in_hbm=(), scratch=(), aliases=()):
    specs = in_smem(len(scalars)) + in_vmem(len(operands))
    operands = list(operands)
    for at in in_hbm:
        specs[len(scalars) + at] = pl.BlockSpec(memory_space=pltpu.HBM)
        operands[at] = pltpu.with_memory_space_constraint(operands[at], pltpu.HBM)
    return pl.pallas_call(
        kernel,
        out_shape=outs,
        in_specs=specs,
        out_specs=in_smem(scalar_outs) + in_vmem(len(outs) - scalar_outs),
        scratch_shapes=scratch,
        input_output_aliases={len(scalars) + taken: given for taken, given in aliases},
        compiler_params=pltpu.CompilerParams(vmem_limit_bytes=vmem_limit),
        cost_estimate=pl.CostEstimate(flops=1000000, bytes_accessed=1000, transcendentals=0),
    )(*scalars, *operands)


def shards(
    forward_state,
    backward_state,
    stored_inputs,
    down_weight,
    up_weight,
    norm_gain,
    latent_gain,
    forward_lengths,
    stored_lengths,
    plan,
):
    sides = stored_inputs.shape[0]
    slot_count, row_count, features = stored_inputs.shape[2:]
    latent_width = down_weight.shape[3]
    tick_count = forward_lengths.shape[2]
    replicas = lax.axis_size("dp")
    columns = features // replicas
    block = slot_count * row_count
    forward_lengths_at = 1
    plan_at = forward_lengths_at + sides * tick_count
    narrow = jnp.bfloat16

    place = (lax.axis_index("pipe") % 2).astype(jnp.int32).reshape(1)

    stored = stored_inputs.reshape(sides, block, features)
    w_down = down_weight[0]
    w_up = up_weight[0]
    gain = norm_gain[0]
    gains_latent = latent_gain[0]

    numbers = (
        jnp.transpose(forward_lengths, (0, 1, 3, 2)),
        plan,
        jnp.transpose(stored_lengths, (0, 1, 3, 2)),
    )

    scalars, normed, to_mirror, *carry = call_kernel(
        functools.partial(prepare_kernel, forward_lengths_at=forward_lengths_at, plan_at=plan_at),
        [
            like(plan_at + sides * tick_count, dtype=jnp.int32),
            like(replicas, block, columns, dtype=narrow),
            like(replicas, block, columns, dtype=narrow),
            like(2 * row_count, features, dtype=narrow),
            like(2 * row_count, features, dtype=narrow),
            like(block, latent_width),
            like(block, latent_width),
            like(sides, block, latent_width, dtype=narrow),
            like(sides, block, latent_width, dtype=narrow),
            like(sides, block, latent_width),
            like(sides, block, 128),
            like(sides, block, 128),
            like(sides, slot_count, row_count, row_count),
        ],
        [place],
        numbers[0],
        numbers[1],
        numbers[2],
        stored,
        forward_state[:, 0],
        backward_state[:, 0],
        w_down,
        gain,
        gains_latent,
        scalar_outs=1,
        in_hbm=range(9),
        scratch=[
            pltpu.VMEM((sides, features, latent_width), narrow),
            pltpu.VMEM(stored.shape, stored.dtype),
            pltpu.VMEM(gain.shape, gain.dtype),
            pltpu.VMEM(gains_latent.shape, gains_latent.dtype),
            *[pltpu.SMEM(array.shape, jnp.int32) for array in numbers],
            pltpu.SemaphoreType.DMA((sides,)),
            pltpu.SemaphoreType.DMA((3,)),
            pltpu.SemaphoreType.DMA((4,)),
            pltpu.SemaphoreType.DMA((3,)),
        ],
    )

    carry, kept = carry[:4], carry[4:]

    def half_step(forward_lane, step, arrived, grads):
        return call_kernel(
            functools.partial(
                half_step_kernel,
                forward_lane=forward_lane,
                lengths_at=forward_lengths_at,
                plan_at=plan_at,
                steps=tick_count,
                step=step,
            ),
            [like(2 * row_count, features, dtype=narrow), like(block, latent_width)],
            [scalars],
            arrived,
            stored,
            w_down,
            w_up,
            gain,
            gains_latent,
            *kept,
            grads,
            aliases=((12, 1),),
        )

    inner, outer, grads_zero, grads_one = carry
    for step in range(tick_count):
        if step == tick_count - 1:
            outer, to_mirror = lax.optimization_barrier((outer, to_mirror))
        to_outer, grads_zero = half_step(1, step, inner, grads_zero)
        to_inner, grads_one = half_step(0, step, outer, grads_one)
        inner = with_chip_partner(to_inner)
        outer = with_outer_partner(to_outer)

    mirrored = from_mirror(to_mirror)
    sums_lower, sums_upper = call_kernel(
        own_grads_kernel,
        [like(block, latent_width, dtype=narrow)] * 2,
        [place],
        grads_zero,
        grads_one,
    )
    sums_mirrored = from_mirror(sums_upper)
    mirrored, sums_mirrored, inner, outer = lax.optimization_barrier(
        (mirrored, sums_mirrored, inner, outer)
    )
    (packed,) = call_kernel(
        pack_kernel,
        [like(replicas, 2 * block, columns + latent_width, dtype=narrow)],
        [],
        normed,
        mirrored,
        sums_lower,
        sums_mirrored,
    )
    packed = lax.all_to_all(packed, "dp", split_axis=0, concat_axis=0, tiled=True)
    (grad_down,) = call_kernel(product_kernel, [like(columns, latent_width)], [], packed)
    forward_out, backward_out = call_kernel(
        own_states_kernel,
        [like(2, row_count, features, dtype=narrow)] * 2,
        [place],
        inner,
        outer,
    )
    return (forward_out[:, None], backward_out[:, None], grad_down[None])


def solution(mesh):
    in_specs = (
        P(None, "pipe", "dp", None),
        P(None, "pipe", "dp", None),
        P(None, "pipe", None, "dp", None),
        P("pipe", None, None, None),
        P("pipe", None, None, None),
        P("pipe", None, None),
        P("pipe", None, None, None),
        P(None, "pipe", None, "dp"),
        P(None, "pipe", None, "dp"),
        P(None, "pipe", None),
    )
    out_specs = (P(None, "pipe", "dp", None), P(None, "pipe", "dp", None), P("pipe", "dp", None))
    return jax.shard_map(shards, mesh=mesh, in_specs=in_specs, out_specs=out_specs, check_vma=False)
```

```python
import functools

import jax
import jax.numpy as jnp
from jax import lax
from jax.experimental import pallas as pl
from jax.experimental.pallas import tpu as pltpu
from jax.sharding import PartitionSpec as P

epsilon = 1e-06
score_factor = 2.0
vmem_limit = 12 * 1024 * 1024


def with_chip_partner(block):
    count = lax.axis_size("pipe")
    return lax.ppermute(block, "pipe", [(i, i ^ 1) for i in range(count)])


def with_outer_partner(block):
    count = lax.axis_size("pipe")
    pairs = []
    for low in range(1, count - 1, 2):
        pairs += [(low, low + 1), (low + 1, low)]
    return lax.ppermute(block, "pipe", pairs)


def from_mirror(block):
    count = lax.axis_size("pipe")
    return lax.ppermute(block, "pipe", [(i, count - 1 - i) for i in range(count)])


def contract(left, right, left_dim, right_dim):
    return lax.dot_general(
        left, right, (((left_dim,), (right_dim,)), ((), ())), preferred_element_type=jnp.float32
    )


def inverse_rms(values):
    return lax.rsqrt(jnp.mean(values * values, axis=-1, keepdims=True) + epsilon)


def probabilities_of(query_rows, key_rows, length):
    row_count, width = query_rows.shape
    scores = contract(query_rows, key_rows, 1, 1) * (score_factor / width)
    query_at = lax.broadcasted_iota(jnp.int32, (row_count, row_count), 0)
    key_at = lax.broadcasted_iota(jnp.int32, (row_count, row_count), 1)
    visible = (key_at <= query_at) & (key_at < length)
    weights = jnp.where(visible, jnp.exp(scores), 0.0)
    return weights / jnp.sum(weights, axis=-1, keepdims=True)


def prepare_kernel(
    place,
    forward_lengths,
    plan,
    stored_lengths,
    stored,
    forward_state,
    backward_state,
    w_down,
    gain,
    latent_gain,
    scalars_out,
    normed_out,
    to_mirror_out,
    inner_out,
    outer_out,
    grads_zero_out,
    grads_one_out,
    key_out,
    query_out,
    unit_out,
    latent_inverse_out,
    input_inverse_out,
    probabilities_out,
    weights,
    stored_here,
    gain_here,
    latent_gain_here,
    forward_lengths_here,
    plan_here,
    stored_lengths_here,
    weights_arrived,
    inputs_arrived,
    states_arrived,
    numbers_arrived,
    *,
    forward_lengths_at,
    plan_at,
):
    sides, slots, row_count = probabilities_out.shape[:3]
    replicas, block, columns = normed_out.shape
    steps = plan.shape[2]
    core = place[0]
    copies = [
        pltpu.make_async_copy(w_down.at[side], weights.at[side], weights_arrived.at[side])
        for side in range(sides)
    ]
    inputs = [
        pltpu.make_async_copy(source, target, inputs_arrived.at[at])
        for at, (source, target) in enumerate(
            ((gain, gain_here), (stored, stored_here), (latent_gain, latent_gain_here))
        )
    ]
    others = [
        pltpu.make_async_copy(source, target, numbers_arrived.at[at])
        for at, (source, target) in enumerate(
            (
                (forward_lengths, forward_lengths_here),
                (plan, plan_here),
                (stored_lengths, stored_lengths_here),
            )
        )
    ]
    others += [
        pltpu.make_async_copy(source.at[side], target, states_arrived.at[at])
        for at, (source, side, target) in enumerate(
            (
                (forward_state, 1 - core, inner_out.at[0:row_count]),
                (backward_state, core, inner_out.at[row_count : 2 * row_count]),
                (forward_state, core, outer_out.at[0:row_count]),
                (backward_state, 1 - core, outer_out.at[row_count : 2 * row_count]),
            )
        )
    ]
    for copy in inputs + copies + others:
        copy.start()
    grads_zero_out[...] = jnp.zeros(grads_zero_out.shape, grads_zero_out.dtype)
    grads_one_out[...] = jnp.zeros(grads_one_out.shape, grads_one_out.dtype)
    for copy in inputs:
        copy.wait()
    all_normed = []
    for side in range(sides):
        rows = stored_here[side].astype(jnp.float32)
        inverse = inverse_rms(rows)
        input_inverse_out[side] = jnp.broadcast_to(inverse, input_inverse_out.shape[1:])
        normed = (rows * inverse * gain_here[side : side + 1]).astype(jnp.bfloat16)
        all_normed.append(normed)
        if side == 1:
            to_mirror_out[...] = normed
            continue
        for replica in range(replicas):
            normed_out[replica] = normed[:, replica * columns : (replica + 1) * columns]
    for copy in others:
        copy.wait()
    scalars_out[0] = core
    for side in range(sides):
        for step in range(steps):
            scalars_out[forward_lengths_at + side * steps + step] = forward_lengths_here[
                side, 0, 0, step
            ]
            scalars_out[plan_at + side * steps + step] = plan_here[side, 0, step]
    for side in range(sides):
        copies[side].wait()
        latent = jnp.dot(all_normed[side], weights[side], preferred_element_type=jnp.float32)
        inverse = inverse_rms(latent)
        unit = latent * inverse
        key_rows = (unit * latent_gain_here[side, 0:1]).astype(jnp.bfloat16)
        query_rows = (unit * latent_gain_here[side, 1:2]).astype(jnp.bfloat16)
        latent_inverse_out[side] = jnp.broadcast_to(inverse, latent_inverse_out.shape[1:])
        unit_out[side] = unit
        key_out[side] = key_rows
        query_out[side] = query_rows
        for slot in range(slots):
            part = slice(slot * row_count, (slot + 1) * row_count)
            probabilities_out[side, slot] = probabilities_of(
                query_rows[part], key_rows[part], stored_lengths_here[side, 0, 0, slot]
            )


def normed_rows(rows, gain_row):
    return (rows * inverse_rms(rows) * gain_row).astype(jnp.bfloat16)


def forward_ended(rows, latent, side, length, w_up, latent_gain):
    unit = latent * inverse_rms(latent)
    gains = latent_gain[side]
    key_rows = (unit * gains[0:1]).astype(jnp.bfloat16)
    query_rows = (unit * gains[1:2]).astype(jnp.bfloat16)
    weights = probabilities_of(query_rows, key_rows, length).astype(jnp.bfloat16)
    mixed_rows = jnp.dot(weights, key_rows, preferred_element_type=jnp.float32)
    update = jnp.dot(
        mixed_rows.astype(jnp.bfloat16), w_up[side], preferred_element_type=jnp.float32
    )
    return (rows + update).astype(jnp.bfloat16)


def grad_latent_of(grad_mixed, side, slot, latent_gain, kept):
    keys, queries, units, latent_inverses, _, probabilities = kept
    row_count = grad_mixed.shape[0]
    mine = pl.ds(pl.multiple_of(slot * row_count, row_count), row_count)
    key_rows = keys[side, mine]
    query_rows = queries[side, mine]
    weights = probabilities[side, slot]
    gains = latent_gain[side]
    grad_mixed = grad_mixed.astype(jnp.bfloat16)
    grad_weights = contract(grad_mixed, key_rows, 1, 1)
    grad_scores = weights * (
        grad_weights - jnp.sum(grad_weights * weights, axis=-1, keepdims=True)
    )
    grad_scores = (grad_scores * (score_factor / key_rows.shape[1])).astype(jnp.bfloat16)
    grad_query = contract(grad_scores, key_rows, 1, 0)
    grad_key = contract(weights.astype(jnp.bfloat16), grad_mixed, 0, 0) + contract(
        grad_scores, query_rows, 0, 0
    )
    grad_unit = grad_key * gains[0:1] + grad_query * gains[1:2]
    unit = units[side, mine]
    return (
        latent_inverses[side, mine][:, 0:1]
        * (grad_unit - unit * jnp.mean(grad_unit * unit, axis=-1, keepdims=True))
    ).astype(jnp.bfloat16)


def backward_ended(grad_out, grad_latent, side, slot, stored, w_down, gain, kept):
    row_count = grad_out.shape[0]
    mine = pl.ds(pl.multiple_of(slot * row_count, row_count), row_count)
    grad_normed = contract(grad_latent, w_down[side], 1, 1)
    inverse = kept[4][side, mine][:, 0:1]
    unit = stored[side, mine].astype(jnp.float32) * inverse
    grad_unit = grad_normed * gain[pl.ds(side, 1)]
    grad_rows = inverse * (grad_unit - unit * jnp.mean(grad_unit * unit, axis=-1, keepdims=True))
    return (grad_out.astype(jnp.float32) + grad_rows).astype(jnp.bfloat16)


def of_slot(grad_latent, slot, slots):
    grad_latent = grad_latent.astype(jnp.float32)
    return jnp.concatenate(
        [jnp.where(slot == at, grad_latent, 0.0) for at in range(slots)], axis=0
    )


def half_step_kernel(
    scalars,
    arrived,
    stored,
    w_down,
    w_up,
    gain,
    latent_gain,
    *refs,
    forward_lane,
    lengths_at,
    plan_at,
    steps,
    step,
):
    kept, (grads_in, outgoing, grads_out) = refs[:6], refs[6:]
    row_count = outgoing.shape[0] // 2
    core = scalars[0]
    forward_side = forward_lane ^ core
    backward_side = 1 - forward_side
    slot = scalars[plan_at + backward_side * steps + step]
    length = scalars[lengths_at + forward_side * steps + step]
    rows = arrived[0:row_count].astype(jnp.float32)
    grad_out = arrived[row_count:]

    grad_mixed = contract(grad_out, w_up[backward_side], 1, 1)
    normed = normed_rows(rows, gain[pl.ds(forward_side, 1)])
    latent = jnp.dot(normed, w_down[forward_side], preferred_element_type=jnp.float32)
    grad_latent = grad_latent_of(grad_mixed, backward_side, slot, latent_gain, kept)
    grads_out[...] = grads_in[...] + of_slot(grad_latent, slot, grads_out.shape[0] // row_count)
    outgoing[0:row_count] = forward_ended(rows, latent, forward_side, length, w_up, latent_gain)
    outgoing[row_count:] = backward_ended(
        grad_out, grad_latent, backward_side, slot, stored, w_down, gain, kept
    )


def factors_kernel(place, grads_zero, grads_one, rows_upper, lower, upper):
    first = place[0] == 0
    features = rows_upper.shape[1]
    lower[...] = jnp.where(first, grads_zero[...], grads_one[...]).astype(lower.dtype)
    upper[:, :features] = rows_upper[...]
    upper[:, features:] = jnp.where(first, grads_one[...], grads_zero[...]).astype(upper.dtype)


def own_states_kernel(place, inner, outer, forward_out, backward_out):
    core = place[0]
    row_count = forward_out.shape[1]
    forward_out[core] = outer[0:row_count]
    forward_out[1 - core] = inner[0:row_count]
    backward_out[core] = inner[row_count:]
    backward_out[1 - core] = outer[row_count:]


def pack_kernel(rows_lower, grads_lower, upper, packed):
    replicas, block, columns = rows_lower.shape
    grads_upper = upper[:, replicas * columns :]
    for replica in range(replicas):
        packed[replica, 0:block] = jnp.concatenate([rows_lower[replica], grads_lower[...]], axis=1)
        packed[replica, block:] = jnp.concatenate(
            [upper[:, replica * columns : (replica + 1) * columns], grads_upper], axis=1
        )


def product_kernel(packed, result):
    replicas, block, width = packed.shape
    columns = result.shape[0]
    packed = packed[...].reshape(replicas * block, width)
    result[...] = contract(packed[:, :columns], packed[:, columns:], 0, 0)


def in_vmem(count):
    return [pl.BlockSpec(memory_space=pltpu.VMEM)] * count


def in_smem(count):
    return [pl.BlockSpec(memory_space=pltpu.SMEM)] * count


def like(*shape, dtype=jnp.float32):
    return jax.ShapeDtypeStruct(shape, dtype)


def call_kernel(
    kernel, outs, scalars, *operands, scalar_outs=0, in_hbm=(), scratch=(), aliases=(), moved=1000
):
    specs = in_smem(len(scalars)) + in_vmem(len(operands))
    operands = list(operands)
    for at in in_hbm:
        specs[len(scalars) + at] = pl.BlockSpec(memory_space=pltpu.HBM)
        operands[at] = pltpu.with_memory_space_constraint(operands[at], pltpu.HBM)
    return pl.pallas_call(
        kernel,
        out_shape=outs,
        in_specs=specs,
        out_specs=in_smem(scalar_outs) + in_vmem(len(outs) - scalar_outs),
        scratch_shapes=scratch,
        input_output_aliases={len(scalars) + taken: given for taken, given in aliases},
        compiler_params=pltpu.CompilerParams(vmem_limit_bytes=vmem_limit),
        cost_estimate=pl.CostEstimate(flops=1000000, bytes_accessed=moved, transcendentals=0),
    )(*scalars, *operands)


def shards(
    forward_state,
    backward_state,
    stored_inputs,
    down_weight,
    up_weight,
    norm_gain,
    latent_gain,
    forward_lengths,
    stored_lengths,
    plan,
):
    sides = stored_inputs.shape[0]
    slot_count, row_count, features = stored_inputs.shape[2:]
    latent_width = down_weight.shape[3]
    tick_count = forward_lengths.shape[2]
    replicas = lax.axis_size("dp")
    columns = features // replicas
    block = slot_count * row_count
    forward_lengths_at = 1
    plan_at = forward_lengths_at + sides * tick_count
    narrow = jnp.bfloat16

    place = (lax.axis_index("pipe") % 2).astype(jnp.int32).reshape(1)

    stored = stored_inputs.reshape(sides, block, features)
    w_down = down_weight[0]
    w_up = up_weight[0]
    gain = norm_gain[0]
    gains_latent = latent_gain[0]

    numbers = (
        jnp.transpose(forward_lengths, (0, 1, 3, 2)),
        plan,
        jnp.transpose(stored_lengths, (0, 1, 3, 2)),
    )

    scalars, normed, to_mirror, *carry = call_kernel(
        functools.partial(prepare_kernel, forward_lengths_at=forward_lengths_at, plan_at=plan_at),
        [
            like(plan_at + sides * tick_count, dtype=jnp.int32),
            like(replicas, block, columns, dtype=narrow),
            like(block, features, dtype=narrow),
            like(2 * row_count, features, dtype=narrow),
            like(2 * row_count, features, dtype=narrow),
            like(block, latent_width),
            like(block, latent_width),
            like(sides, block, latent_width, dtype=narrow),
            like(sides, block, latent_width, dtype=narrow),
            like(sides, block, latent_width),
            like(sides, block, 128),
            like(sides, block, 128),
            like(sides, slot_count, row_count, row_count),
        ],
        [place],
        numbers[0],
        numbers[1],
        numbers[2],
        stored,
        forward_state[:, 0],
        backward_state[:, 0],
        w_down,
        gain,
        gains_latent,
        scalar_outs=1,
        in_hbm=range(9),
        moved=12000000,
        scratch=[
            pltpu.VMEM((sides, features, latent_width), narrow),
            pltpu.VMEM(stored.shape, stored.dtype),
            pltpu.VMEM(gain.shape, gain.dtype),
            pltpu.VMEM(gains_latent.shape, gains_latent.dtype),
            *[pltpu.SMEM(array.shape, jnp.int32) for array in numbers],
            pltpu.SemaphoreType.DMA((sides,)),
            pltpu.SemaphoreType.DMA((3,)),
            pltpu.SemaphoreType.DMA((4,)),
            pltpu.SemaphoreType.DMA((3,)),
        ],
    )

    carry, kept = carry[:4], carry[4:]

    def half_step(forward_lane, step, arrived, grads):
        return call_kernel(
            functools.partial(
                half_step_kernel,
                forward_lane=forward_lane,
                lengths_at=forward_lengths_at,
                plan_at=plan_at,
                steps=tick_count,
                step=step,
            ),
            [like(2 * row_count, features, dtype=narrow), like(block, latent_width)],
            [scalars],
            arrived,
            stored,
            w_down,
            w_up,
            gain,
            gains_latent,
            *kept,
            grads,
            aliases=((12, 1),),
        )

    inner, outer, grads_zero, grads_one = carry
    for step in range(tick_count):
        to_outer, grads_zero = half_step(1, step, inner, grads_zero)
        to_inner, grads_one = half_step(0, step, outer, grads_one)
        if step < tick_count - 1:
            inner = with_chip_partner(to_inner)
            outer = with_outer_partner(to_outer)

    sums_lower, upper = call_kernel(
        factors_kernel,
        [
            like(block, latent_width, dtype=narrow),
            like(block, features + latent_width, dtype=narrow),
        ],
        [place],
        grads_zero,
        grads_one,
        to_mirror,
    )
    upper = from_mirror(upper)

    (packed,) = call_kernel(
        pack_kernel,
        [like(replicas, 2 * block, columns + latent_width, dtype=narrow)],
        [],
        normed,
        sums_lower,
        upper,
    )
    inner = with_chip_partner(to_inner)
    outer = with_outer_partner(to_outer)
    packed, inner, outer = lax.optimization_barrier((packed, inner, outer))
    packed = lax.all_to_all(packed, "dp", split_axis=0, concat_axis=0, tiled=True)
    (grad_down,) = call_kernel(product_kernel, [like(columns, latent_width)], [], packed)
    forward_out, backward_out = call_kernel(
        own_states_kernel,
        [like(2, row_count, features, dtype=narrow)] * 2,
        [place],
        inner,
        outer,
    )
    return (forward_out[:, None], backward_out[:, None], grad_down[None])


def solution(mesh):
    in_specs = (
        P(None, "pipe", "dp", None),
        P(None, "pipe", "dp", None),
        P(None, "pipe", None, "dp", None),
        P("pipe", None, None, None),
        P("pipe", None, None, None),
        P("pipe", None, None),
        P("pipe", None, None, None),
        P(None, "pipe", None, "dp"),
        P(None, "pipe", None, "dp"),
        P(None, "pipe", None),
    )
    out_specs = (P(None, "pipe", "dp", None), P(None, "pipe", "dp", None), P("pipe", "dp", None))
    return jax.shard_map(shards, mesh=mesh, in_specs=in_specs, out_specs=out_specs, check_vma=False)
```

```python
import functools

import jax
import jax.numpy as jnp
from jax import lax
from jax.experimental import pallas as pl
from jax.experimental.pallas import tpu as pltpu
from jax.sharding import PartitionSpec as P

epsilon = 1e-06
score_factor = 2.0
vmem_limit = 12 * 1024 * 1024


def with_chip_partner(block):
    count = lax.axis_size("pipe")
    return lax.ppermute(block, "pipe", [(i, i ^ 1) for i in range(count)])


def with_outer_partner(block):
    count = lax.axis_size("pipe")
    pairs = []
    for low in range(1, count - 1, 2):
        pairs += [(low, low + 1), (low + 1, low)]
    return lax.ppermute(block, "pipe", pairs)


def from_mirror(block):
    count = lax.axis_size("pipe")
    return lax.ppermute(block, "pipe", [(i, count - 1 - i) for i in range(count)])


def contract(left, right, left_dim, right_dim):
    return lax.dot_general(
        left, right, (((left_dim,), (right_dim,)), ((), ())), preferred_element_type=jnp.float32
    )


def inverse_rms(values):
    return lax.rsqrt(jnp.mean(values * values, axis=-1, keepdims=True) + epsilon)


def probabilities_of(query_rows, key_rows, length):
    row_count, width = query_rows.shape
    scores = contract(query_rows, key_rows, 1, 1) * (score_factor / width)
    query_at = lax.broadcasted_iota(jnp.int32, (row_count, row_count), 0)
    key_at = lax.broadcasted_iota(jnp.int32, (row_count, row_count), 1)
    visible = (key_at <= query_at) & (key_at < length)
    weights = jnp.where(visible, jnp.exp(scores), 0.0)
    return weights / jnp.sum(weights, axis=-1, keepdims=True)


def prepare_kernel(
    place,
    forward_lengths,
    plan,
    stored_lengths,
    stored,
    forward_state,
    backward_state,
    w_down,
    w_up,
    gain,
    latent_gain,
    scalars_out,
    weights,
    up_out,
    normed_out,
    to_mirror_out,
    inner_out,
    outer_out,
    grads_zero_out,
    grads_one_out,
    key_out,
    query_out,
    unit_out,
    latent_inverse_out,
    input_inverse_out,
    probabilities_out,
    stored_here,
    gain_here,
    latent_gain_here,
    forward_lengths_here,
    plan_here,
    stored_lengths_here,
    weights_arrived,
    inputs_arrived,
    states_arrived,
    numbers_arrived,
    up_arrived,
    *,
    forward_lengths_at,
    plan_at,
):
    sides, slots, row_count = probabilities_out.shape[:3]
    replicas, block, columns = normed_out.shape
    steps = plan.shape[2]
    core = place[0]
    copies = [
        pltpu.make_async_copy(w_down.at[side], weights.at[side], weights_arrived.at[side])
        for side in range(sides)
    ]
    later = pltpu.make_async_copy(w_up, up_out, up_arrived)
    inputs = [
        pltpu.make_async_copy(source, target, inputs_arrived.at[at])
        for at, (source, target) in enumerate(
            ((gain, gain_here), (stored, stored_here), (latent_gain, latent_gain_here))
        )
    ]
    others = [
        pltpu.make_async_copy(source, target, numbers_arrived.at[at])
        for at, (source, target) in enumerate(
            (
                (forward_lengths, forward_lengths_here),
                (plan, plan_here),
                (stored_lengths, stored_lengths_here),
            )
        )
    ]
    others += [
        pltpu.make_async_copy(source.at[side], target, states_arrived.at[at])
        for at, (source, side, target) in enumerate(
            (
                (forward_state, 1 - core, inner_out.at[0:row_count]),
                (backward_state, core, inner_out.at[row_count : 2 * row_count]),
                (forward_state, core, outer_out.at[0:row_count]),
                (backward_state, 1 - core, outer_out.at[row_count : 2 * row_count]),
            )
        )
    ]
    for copy in inputs + copies + others + [later]:
        copy.start()
    grads_zero_out[...] = jnp.zeros(grads_zero_out.shape, grads_zero_out.dtype)
    grads_one_out[...] = jnp.zeros(grads_one_out.shape, grads_one_out.dtype)
    for copy in inputs:
        copy.wait()
    all_normed = []
    for side in range(sides):
        rows = stored_here[side].astype(jnp.float32)
        inverse = inverse_rms(rows)
        input_inverse_out[side] = jnp.broadcast_to(inverse, input_inverse_out.shape[1:])
        normed = (rows * inverse * gain_here[side : side + 1]).astype(jnp.bfloat16)
        all_normed.append(normed)
        if side == 1:
            to_mirror_out[...] = normed
            continue
        for replica in range(replicas):
            normed_out[replica] = normed[:, replica * columns : (replica + 1) * columns]
    for copy in others:
        copy.wait()
    scalars_out[0] = core
    for side in range(sides):
        for step in range(steps):
            scalars_out[forward_lengths_at + side * steps + step] = forward_lengths_here[
                side, 0, 0, step
            ]
            scalars_out[plan_at + side * steps + step] = plan_here[side, 0, step]
    for side in range(sides):
        copies[side].wait()
        latent = jnp.dot(all_normed[side], weights[side], preferred_element_type=jnp.float32)
        inverse = inverse_rms(latent)
        unit = latent * inverse
        key_rows = (unit * latent_gain_here[side, 0:1]).astype(jnp.bfloat16)
        query_rows = (unit * latent_gain_here[side, 1:2]).astype(jnp.bfloat16)
        latent_inverse_out[side] = jnp.broadcast_to(inverse, latent_inverse_out.shape[1:])
        unit_out[side] = unit
        key_out[side] = key_rows
        query_out[side] = query_rows
        for slot in range(slots):
            part = slice(slot * row_count, (slot + 1) * row_count)
            probabilities_out[side, slot] = probabilities_of(
                query_rows[part], key_rows[part], stored_lengths_here[side, 0, 0, slot]
            )
    later.wait()


def normed_rows(rows, gain_row):
    return (rows * inverse_rms(rows) * gain_row).astype(jnp.bfloat16)


def forward_ended(rows, latent, side, length, w_up, latent_gain):
    unit = latent * inverse_rms(latent)
    gains = latent_gain[side]
    key_rows = (unit * gains[0:1]).astype(jnp.bfloat16)
    query_rows = (unit * gains[1:2]).astype(jnp.bfloat16)
    weights = probabilities_of(query_rows, key_rows, length).astype(jnp.bfloat16)
    mixed_rows = jnp.dot(weights, key_rows, preferred_element_type=jnp.float32)
    update = jnp.dot(
        mixed_rows.astype(jnp.bfloat16), w_up[side], preferred_element_type=jnp.float32
    )
    return (rows + update).astype(jnp.bfloat16)


def grad_latent_of(grad_mixed, side, slot, latent_gain, kept):
    keys, queries, units, latent_inverses, _, probabilities = kept
    row_count = grad_mixed.shape[0]
    mine = pl.ds(pl.multiple_of(slot * row_count, row_count), row_count)
    key_rows = keys[side, mine]
    query_rows = queries[side, mine]
    weights = probabilities[side, slot]
    gains = latent_gain[side]
    grad_mixed = grad_mixed.astype(jnp.bfloat16)
    grad_weights = contract(grad_mixed, key_rows, 1, 1)
    grad_scores = weights * (
        grad_weights - jnp.sum(grad_weights * weights, axis=-1, keepdims=True)
    )
    grad_scores = (grad_scores * (score_factor / key_rows.shape[1])).astype(jnp.bfloat16)
    grad_query = contract(grad_scores, key_rows, 1, 0)
    grad_key = contract(weights.astype(jnp.bfloat16), grad_mixed, 0, 0) + contract(
        grad_scores, query_rows, 0, 0
    )
    grad_unit = grad_key * gains[0:1] + grad_query * gains[1:2]
    unit = units[side, mine]
    return (
        latent_inverses[side, mine][:, 0:1]
        * (grad_unit - unit * jnp.mean(grad_unit * unit, axis=-1, keepdims=True))
    ).astype(jnp.bfloat16)


def backward_ended(grad_out, grad_latent, side, slot, stored, w_down, gain, kept):
    row_count = grad_out.shape[0]
    mine = pl.ds(pl.multiple_of(slot * row_count, row_count), row_count)
    grad_normed = contract(grad_latent, w_down[side], 1, 1)
    inverse = kept[4][side, mine][:, 0:1]
    unit = stored[side, mine].astype(jnp.float32) * inverse
    grad_unit = grad_normed * gain[pl.ds(side, 1)]
    grad_rows = inverse * (grad_unit - unit * jnp.mean(grad_unit * unit, axis=-1, keepdims=True))
    return (grad_out.astype(jnp.float32) + grad_rows).astype(jnp.bfloat16)


def of_slot(grad_latent, slot, slots):
    grad_latent = grad_latent.astype(jnp.float32)
    return jnp.concatenate(
        [jnp.where(slot == at, grad_latent, 0.0) for at in range(slots)], axis=0
    )


def half_step_kernel(
    scalars,
    arrived,
    stored,
    w_down,
    w_up,
    gain,
    latent_gain,
    *refs,
    forward_lane,
    lengths_at,
    plan_at,
    steps,
    step,
):
    kept, (grads_in, outgoing, grads_out) = refs[:6], refs[6:]
    row_count = outgoing.shape[0] // 2
    core = scalars[0]
    forward_side = forward_lane ^ core
    backward_side = 1 - forward_side
    slot = scalars[plan_at + backward_side * steps + step]
    length = scalars[lengths_at + forward_side * steps + step]
    rows = arrived[0:row_count].astype(jnp.float32)
    grad_out = arrived[row_count:]

    grad_mixed = contract(grad_out, w_up[backward_side], 1, 1)
    normed = normed_rows(rows, gain[pl.ds(forward_side, 1)])
    latent = jnp.dot(normed, w_down[forward_side], preferred_element_type=jnp.float32)
    grad_latent = grad_latent_of(grad_mixed, backward_side, slot, latent_gain, kept)
    grads_out[...] = grads_in[...] + of_slot(grad_latent, slot, grads_out.shape[0] // row_count)
    outgoing[0:row_count] = forward_ended(rows, latent, forward_side, length, w_up, latent_gain)
    outgoing[row_count:] = backward_ended(
        grad_out, grad_latent, backward_side, slot, stored, w_down, gain, kept
    )


def factors_kernel(place, grads_zero, grads_one, rows_upper, lower, upper):
    first = place[0] == 0
    features = rows_upper.shape[1]
    lower[...] = jnp.where(first, grads_zero[...], grads_one[...]).astype(lower.dtype)
    upper[:, :features] = rows_upper[...]
    upper[:, features:] = jnp.where(first, grads_one[...], grads_zero[...]).astype(upper.dtype)


def own_states_kernel(place, inner, outer, forward_out, backward_out):
    core = place[0]
    row_count = forward_out.shape[1]
    forward_out[core] = outer[0:row_count]
    forward_out[1 - core] = inner[0:row_count]
    backward_out[core] = inner[row_count:]
    backward_out[1 - core] = outer[row_count:]


def pack_kernel(rows_lower, grads_lower, upper, packed):
    replicas, block, columns = rows_lower.shape
    grads_upper = upper[:, replicas * columns :]
    for replica in range(replicas):
        packed[replica, 0:block] = jnp.concatenate([rows_lower[replica], grads_lower[...]], axis=1)
        packed[replica, block:] = jnp.concatenate(
            [upper[:, replica * columns : (replica + 1) * columns], grads_upper], axis=1
        )


def product_kernel(packed, result):
    replicas, block, width = packed.shape
    columns = result.shape[0]
    packed = packed[...].reshape(replicas * block, width)
    result[...] = contract(packed[:, :columns], packed[:, columns:], 0, 0)


def in_vmem(count):
    return [pl.BlockSpec(memory_space=pltpu.VMEM)] * count


def in_smem(count):
    return [pl.BlockSpec(memory_space=pltpu.SMEM)] * count


def like(*shape, dtype=jnp.float32):
    return jax.ShapeDtypeStruct(shape, dtype)


def call_kernel(
    kernel, outs, scalars, *operands, scalar_outs=0, in_hbm=(), scratch=(), aliases=(), moved=1000
):
    specs = in_smem(len(scalars)) + in_vmem(len(operands))
    operands = list(operands)
    for at in in_hbm:
        specs[len(scalars) + at] = pl.BlockSpec(memory_space=pltpu.HBM)
        operands[at] = pltpu.with_memory_space_constraint(operands[at], pltpu.HBM)
    return pl.pallas_call(
        kernel,
        out_shape=outs,
        in_specs=specs,
        out_specs=in_smem(scalar_outs) + in_vmem(len(outs) - scalar_outs),
        scratch_shapes=scratch,
        input_output_aliases={len(scalars) + taken: given for taken, given in aliases},
        compiler_params=pltpu.CompilerParams(vmem_limit_bytes=vmem_limit),
        cost_estimate=pl.CostEstimate(flops=1000000, bytes_accessed=moved, transcendentals=0),
    )(*scalars, *operands)


def shards(
    forward_state,
    backward_state,
    stored_inputs,
    down_weight,
    up_weight,
    norm_gain,
    latent_gain,
    forward_lengths,
    stored_lengths,
    plan,
):
    sides = stored_inputs.shape[0]
    slot_count, row_count, features = stored_inputs.shape[2:]
    latent_width = down_weight.shape[3]
    tick_count = forward_lengths.shape[2]
    replicas = lax.axis_size("dp")
    columns = features // replicas
    block = slot_count * row_count
    forward_lengths_at = 1
    plan_at = forward_lengths_at + sides * tick_count
    narrow = jnp.bfloat16

    place = (lax.axis_index("pipe") % 2).astype(jnp.int32).reshape(1)

    stored = stored_inputs.reshape(sides, block, features)
    w_down = down_weight[0]
    w_up = up_weight[0]
    gain = norm_gain[0]
    gains_latent = latent_gain[0]

    numbers = (
        jnp.transpose(forward_lengths, (0, 1, 3, 2)),
        plan,
        jnp.transpose(stored_lengths, (0, 1, 3, 2)),
    )

    scalars, down_here, up_here, normed, to_mirror, *carry = call_kernel(
        functools.partial(prepare_kernel, forward_lengths_at=forward_lengths_at, plan_at=plan_at),
        [
            like(plan_at + sides * tick_count, dtype=jnp.int32),
            like(*w_down.shape, dtype=narrow),
            like(*w_up.shape, dtype=narrow),
            like(replicas, block, columns, dtype=narrow),
            like(block, features, dtype=narrow),
            like(2 * row_count, features, dtype=narrow),
            like(2 * row_count, features, dtype=narrow),
            like(block, latent_width),
            like(block, latent_width),
            like(sides, block, latent_width, dtype=narrow),
            like(sides, block, latent_width, dtype=narrow),
            like(sides, block, latent_width),
            like(sides, block, 128),
            like(sides, block, 128),
            like(sides, slot_count, row_count, row_count),
        ],
        [place],
        numbers[0],
        numbers[1],
        numbers[2],
        stored,
        forward_state[:, 0],
        backward_state[:, 0],
        w_down,
        w_up,
        gain,
        gains_latent,
        scalar_outs=1,
        in_hbm=range(10),
        moved=12000000,
        scratch=[
            pltpu.VMEM(stored.shape, stored.dtype),
            pltpu.VMEM(gain.shape, gain.dtype),
            pltpu.VMEM(gains_latent.shape, gains_latent.dtype),
            *[pltpu.SMEM(array.shape, jnp.int32) for array in numbers],
            pltpu.SemaphoreType.DMA((sides,)),
            pltpu.SemaphoreType.DMA((3,)),
            pltpu.SemaphoreType.DMA((4,)),
            pltpu.SemaphoreType.DMA((3,)),
            pltpu.SemaphoreType.DMA,
        ],
    )

    carry, kept = carry[:4], carry[4:]

    def half_step(forward_lane, step, arrived, grads):
        return call_kernel(
            functools.partial(
                half_step_kernel,
                forward_lane=forward_lane,
                lengths_at=forward_lengths_at,
                plan_at=plan_at,
                steps=tick_count,
                step=step,
            ),
            [like(2 * row_count, features, dtype=narrow), like(block, latent_width)],
            [scalars],
            arrived,
            stored,
            down_here,
            up_here,
            gain,
            gains_latent,
            *kept,
            grads,
            aliases=((12, 1),),
        )

    inner, outer, grads_zero, grads_one = carry
    for step in range(tick_count):
        to_outer, grads_zero = half_step(1, step, inner, grads_zero)
        to_inner, grads_one = half_step(0, step, outer, grads_one)
        if step < tick_count - 1:
            inner = with_chip_partner(to_inner)
            outer = with_outer_partner(to_outer)

    sums_lower, upper = call_kernel(
        factors_kernel,
        [
            like(block, latent_width, dtype=narrow),
            like(block, features + latent_width, dtype=narrow),
        ],
        [place],
        grads_zero,
        grads_one,
        to_mirror,
    )
    upper = from_mirror(upper)

    (packed,) = call_kernel(
        pack_kernel,
        [like(replicas, 2 * block, columns + latent_width, dtype=narrow)],
        [],
        normed,
        sums_lower,
        upper,
    )
    inner = with_chip_partner(to_inner)
    outer = with_outer_partner(to_outer)
    packed, inner, outer = lax.optimization_barrier((packed, inner, outer))
    packed = lax.all_to_all(packed, "dp", split_axis=0, concat_axis=0, tiled=True)
    (grad_down,) = call_kernel(product_kernel, [like(columns, latent_width)], [], packed)
    forward_out, backward_out = call_kernel(
        own_states_kernel,
        [like(2, row_count, features, dtype=narrow)] * 2,
        [place],
        inner,
        outer,
    )
    return (forward_out[:, None], backward_out[:, None], grad_down[None])


def solution(mesh):
    in_specs = (
        P(None, "pipe", "dp", None),
        P(None, "pipe", "dp", None),
        P(None, "pipe", None, "dp", None),
        P("pipe", None, None, None),
        P("pipe", None, None, None),
        P("pipe", None, None),
        P("pipe", None, None, None),
        P(None, "pipe", None, "dp"),
        P(None, "pipe", None, "dp"),
        P(None, "pipe", None),
    )
    out_specs = (P(None, "pipe", "dp", None), P(None, "pipe", "dp", None), P("pipe", "dp", None))
    return jax.shard_map(shards, mesh=mesh, in_specs=in_specs, out_specs=out_specs, check_vma=False)
```
